32 devices in a mesh: groups: 2 (over y), gx: 4 (over x, core), gy: 4 (over z).
Axes of the slice: x: 2, y: 2, z: 4, core: 2. Of those that a mesh axis runs over, the one named last changes fastest.
Arguments:
- tokens: bfloat16 [2, 1024, 18432], P(None, 'groups', ('gx', 'gy')), parts along dimension 1, may hold values from -400 to 400
- norm_gain: bfloat16 [18432], P(('gx', 'gy')), may hold values from 0.5 to 1.5
- gate_weight: bfloat16 [18432, 9216], P('gx', 'gy'), may hold values from -0.046875 to 0.046875
- up_weight: bfloat16 [18432, 9216], P('gx', 'gy'), may hold values from -0.046875 to 0.046875
- down_weight: bfloat16 [9216, 18432], P('gy', 'gx'), may hold values from -0.09375 to 0.09375
Outputs:
- ffn_output: bfloat16 [2, 1024, 18432], P(None, 'groups', ('gx', 'gy')), parts along dimension 1
The draws below stay inside these ranges and needn't reach their ends.
There are 2 independent parts, one for each index of `groups`. The reference program is written for one: setup_inputs(seed, part) draws one part's arguments, and reference() takes and returns one part's arrays. A program takes and returns all parts, laid end to end along the dimension named above; an argument that names none is the same for every part. Nothing has to cross between parts.
All inputs are finite; a program needn't handle non-finite values.
Results may differ from the reference program's by a relative error of at most 0.0065.
Values may be sent and summed in bfloat16 or wider, within the bound.
No kernel may reach another device: no remote copies, remote signals or barrier semaphores. Data moves between devices by JAX's collectives and lax.ppermute only.
A program may use at most 192 MiB of HBM per device.

```python
import math
import jax
import jax.numpy as jnp
from jax import lax

D = 18432
FF = 9216
ROWS = 512
MICRO = 2


def draw_tokens(key, part):
    key = jax.random.fold_in(key, 11)
    first, second, third = jax.random.split(key, 3)
    position = jnp.arange(D, dtype=jnp.float32) / D
    column_scale = jnp.power(3.0, position) * jnp.exp(jax.random.uniform(second, (D,), jnp.float32, -1.15, 1.15))
    row_scale = jnp.exp(jax.random.uniform(third, (MICRO, ROWS, 1), jnp.float32, 0.0, math.log(10.0)))
    base = jax.random.truncated_normal(first, -4.0, 4.0, (MICRO, ROWS, D), jnp.float32)
    return (base * row_scale * column_scale).astype(jnp.bfloat16)


def spiked(drawn, key, source, target, shards_of, factor):
    def block_of(dim):
        return (jnp.arange(drawn.shape[dim]) // (drawn.shape[dim] // shards_of)).reshape((-1,) + (1,) * (drawn.ndim - 1 - dim))

    first = jax.random.permutation(key, shards_of)[block_of(target)]
    far = (block_of(target) + shards_of // 2) % shards_of
    return jnp.where((block_of(source) == first) | (block_of(source) == far), factor * drawn, drawn)


def block_levels(key, extent, cuts, least, high):
    loudness = 1.0
    for dim, blocks in cuts:
        heights = jax.random.uniform(jax.random.fold_in(jax.random.fold_in(key, 6), dim), (blocks,), jnp.float32, least / len(cuts), high / len(cuts))
        loudness = loudness * jnp.repeat(jnp.exp(heights), extent[dim] // blocks).reshape((-1,) + (1,) * (len(extent) - 1 - dim))
    return loudness


def centred(stream_key, dims, spread, limit, cuts=(), held_as=jnp.bfloat16):
    array = spread * jax.random.normal(stream_key, dims, jnp.float32)
    if cuts:
        array = array * block_levels(stream_key, dims, cuts, -0.22, 0.18)
    return jnp.clip(array, -limit, limit).astype(held_as)


def gaussian_with(rng, dims, deviation, limit, cuts, heavy, held_as=jnp.bfloat16):
    entries = deviation * jax.random.normal(rng, dims, jnp.float32)
    if cuts:
        entries = entries * block_levels(rng, dims, cuts, -0.22, 0.18)
    return jnp.clip(spiked(entries, jax.random.fold_in(rng, 3), *heavy), -limit, limit).astype(held_as)


def setup_inputs(seed: int = 0, part: int = 0) -> dict:
    key_of = jax.random.split(jax.random.key(seed), 6)
    part_splits = jax.random.split(jax.random.fold_in(key_of[5], part), 6)
    return {
        "tokens": draw_tokens(jax.random.fold_in(jax.random.fold_in(key_of[5], part), 71), part),
        "norm_gain": jnp.clip(0.5 + 1.0 * jax.random.uniform(key_of[1], (D,), jnp.float32) ** block_levels(key_of[1], (D,), ((0, 16),), -0.2, 0.2), 0.5, 1.5).astype(jnp.bfloat16),
        "gate_weight": centred(key_of[2], (D, FF), D ** -0.5, 0.046875, ((0, 4), (1, 4))),
        "up_weight": centred(key_of[3], (D, FF), D ** -0.5, 0.046875, ((0, 4), (1, 4))),
        "down_weight": gaussian_with(key_of[4], (FF, D), FF ** -0.5, 0.09375, ((0, 4), (1, 4)), (0, 1, 4, 2.0)),
    }


epsilon = 1e-05

def reference(tokens, norm_gain, gate_weight, up_weight, down_weight):
    values = tokens.astype(jnp.float32)
    squares = lax.optimization_barrier(jnp.sum(values * values, axis=-1, keepdims=True))
    normed = (values * lax.rsqrt(squares / D + epsilon) * norm_gain.astype(jnp.float32)).astype(jnp.bfloat16)
    results = []
    for micro_index in range(MICRO):
        block = normed[micro_index]
        gate = jnp.dot(block, gate_weight, preferred_element_type=jnp.float32)
        up_sum = jnp.dot(block, up_weight, preferred_element_type=jnp.float32)
        hidden = (jax.nn.silu(gate) * up_sum).astype(jnp.bfloat16)
        results.append(jnp.dot(hidden, down_weight, preferred_element_type=jnp.float32).astype(jnp.bfloat16))
    return jnp.stack(results, axis=0)
```

```python
import functools

import jax
import jax.numpy as jnp
from jax import lax
from jax.experimental import pallas as pl
from jax.experimental.pallas import tpu as pltpu
from jax.sharding import PartitionSpec as P

D = 18432
CORES = 2
CHUNKS = (256, 256, 256, 256)
ORDER = (1, 1, 3, 1, 2, 0, 3, 0, 1, 0, 2, 1, 0, 3, 0, 2, 1, 3, 0, 1, 3, 1, 2, 3, 1, 2, 3, 0, 3, 2, 1, 2, 2, 1, 3, 2, 0, 3, 2, 3, 2)
VMEM = 48 * 1024 * 1024
bf16, f32 = jnp.bfloat16, jnp.float32


epsilon = 1e-05


def rotate(value, axis, count, stride, by):
    pairs = []
    for place in range(count):
        for rest in range(stride):
            pairs.append((place * stride + rest, (place + by) % count * stride + rest))
    return lax.ppermute(value, axis, pairs)


def swap_core(value, size):
    return lax.ppermute(value, "gx", [(i, i ^ 1) for i in range(size)])


def gate_up_kernel(n, first, at, *refs):
    own, up, down = refs[0], refs[1:n], refs[n : 2 * n - 1]
    scale, gain, gate_w, up_w, send_gate, send_up, keep, normed, product = refs[2 * n - 1 :]
    place, core = at[0], at[1]
    width = own.shape[1]
    rows = slice(first, first + own.shape[0])
    half = product.shape[0] // CORES

    @pl.when(pl.program_id(0) == 0)
    def _():
        def fill(t, source):
            column = pl.multiple_of(lax.rem(place + (n - t), n) * width, 128)
            values = source[...].astype(f32) * scale[rows, :] * gain[t : t + 1, :]
            normed[:, pl.ds(column, width)] = values.astype(bf16)

        fill(0, own)
        for t in range(1, n):
            pl.when(place >= t)(functools.partial(fill, t, up[t - 1]))
            pl.when(place < t)(functools.partial(fill, t, down[n - t - 1]))

    for k, (weight, send) in enumerate(((gate_w, send_gate), (up_w, send_up))):
        product[...] = jnp.dot(normed[...], weight[...], preferred_element_type=f32)
        send[...] = product[pl.ds(pl.multiple_of((1 - core) * half, 16), half), :].astype(bf16)
        keep[k] = product[pl.ds(pl.multiple_of(core * half, 16), half), :]


def gate_up(at, first, up, down, scale, gain, gate_weight, up_weight):
    n = len(up)
    rows, width = up[0].shape
    depth, cols = gate_weight.shape
    half = rows // CORES
    if width % 128 or cols % 256:
        place, core = at[0], at[1]
        normed = jnp.zeros((rows, depth), bf16)
        for t in range(n):
            piece = up[0] if t == 0 else jnp.where(place >= t, up[t], down[n - t])
            piece = (piece.astype(f32) * scale[first : first + rows] * gain[t][None, :]).astype(bf16)
            normed = lax.dynamic_update_slice(normed, piece, (0, lax.rem(place + n - t, n) * width))
        both = jnp.stack(
            [jnp.dot(normed, w, preferred_element_type=f32) for w in (gate_weight, up_weight)]
        ).reshape(2, CORES, half, cols)
        pick = lambda c: lax.dynamic_index_in_dim(both, c, 1, keepdims=False)
        away = pick(1 - core).astype(bf16)
        return away[0], away[1], pick(core)
    tile = 256
    whole = lambda shape: pl.BlockSpec(shape, lambda j, at: (0,) * len(shape))
    weight = pl.BlockSpec((depth, tile), lambda j, at: (0, j))
    result = pl.BlockSpec((2, half, tile), lambda j, at: (0, 0, j))
    away = pl.BlockSpec((half, tile), lambda j, at: (0, j))
    return pl.pallas_call(
        functools.partial(gate_up_kernel, n, first),
        grid_spec=pltpu.PrefetchScalarGridSpec(
            num_scalar_prefetch=1,
            grid=(cols // tile,),
            in_specs=[whole((rows, width))] * (2 * n - 1)
            + [whole(scale.shape), whole((n, width)), weight, weight],
            out_specs=[away, away, result],
            scratch_shapes=[pltpu.VMEM((rows, depth), bf16), pltpu.VMEM((rows, tile), f32)],
        ),
        out_shape=[
            jax.ShapeDtypeStruct((half, cols), bf16),
            jax.ShapeDtypeStruct((half, cols), bf16),
            jax.ShapeDtypeStruct((2, half, cols), f32),
        ],
        compiler_params=pltpu.CompilerParams(vmem_limit_bytes=VMEM),
        cost_estimate=pl.CostEstimate(flops=0, bytes_accessed=0, transcendentals=0),
        name="gate_up",
    )(at, *up, *down[1:], scale, gain, gate_weight, up_weight)


def down_kernel(ring, at, *refs):
    mine, other = refs[:ring], refs[ring : 2 * ring]
    weight, terms, ahead, behind, hidden = refs[2 * ring :]
    core, x = at[1], at[2]
    part = mine[0].shape[0]

    @pl.when(pl.program_id(0) == 0)
    def _():
        for c, pieces in ((core, mine), (1 - core, other)):
            for s in range(ring):
                row = (c * ring + lax.rem(x + (ring - s), ring)) * part
                hidden[pl.ds(pl.multiple_of(row, 16), part), :] = pieces[s][...]

    product = jnp.dot(hidden[...], weight[...], preferred_element_type=f32)
    terms[0] = product

    @pl.when(pl.program_id(0) == pl.num_programs(0) - 1)
    def _():
        ahead[...] = product.astype(bf16)

    @pl.when(pl.program_id(0) == 0)
    def _():
        behind[...] = product.astype(bf16)


def down(at, mine, other, down_weight, n):
    ring = len(mine)
    part, depth = mine[0].shape
    rows = part * ring * CORES
    width = down_weight.shape[1] // n
    if width % 128:
        core, x = at[1], at[2]
        hidden = jnp.zeros((rows, depth), bf16)
        for c, pieces in ((core, mine), (1 - core, other)):
            for s in range(ring):
                row = (c * ring + lax.rem(x + ring - s, ring)) * part
                hidden = lax.dynamic_update_slice(hidden, pieces[s], (row, 0))
        terms = jnp.dot(hidden, down_weight, preferred_element_type=f32)
        terms = terms.reshape(rows, n, width).transpose(1, 0, 2)
        return terms, terms[n - 1].astype(bf16), terms[0].astype(bf16)
    return pl.pallas_call(
        functools.partial(down_kernel, ring),
        grid_spec=pltpu.PrefetchScalarGridSpec(
            num_scalar_prefetch=1,
            grid=(n,),
            in_specs=[pl.BlockSpec((part, depth), lambda j, at: (0, 0))] * (2 * ring)
            + [pl.BlockSpec((depth, width), lambda j, at: (0, j))],
            out_specs=[pl.BlockSpec((1, rows, width), lambda j, at: (j, 0, 0))]
            + [pl.BlockSpec((rows, width), lambda j, at: (0, 0))] * 2,
            scratch_shapes=[pltpu.VMEM((rows, depth), bf16)],
        ),
        out_shape=[jax.ShapeDtypeStruct((n, rows, width), f32)]
        + [jax.ShapeDtypeStruct((rows, width), bf16)] * 2,
        compiler_params=pltpu.CompilerParams(vmem_limit_bytes=VMEM),
        cost_estimate=pl.CostEstimate(flops=0, bytes_accessed=0, transcendentals=0),
        name="down",
    )(at, *mine, *other, down_weight)


class Turn:
    def __init__(self):
        self.held = ()

    def take(self, *values):
        values, _ = lax.optimization_barrier((values, self.held))
        self.held = values
        return values

    def give(self, *values):
        self.held = values


def chunk_blocks(turn, gx, n, at, first, size, tokens, notes, weights, outputs):
    gate_weight, up_weight, down_weight = weights
    place, core, x = at[0], at[1], at[2]
    ring = gx // CORES
    part = size // gx

    (shard,) = turn.take(tokens[first : first + size])
    up, back = [shard], [shard]
    for t in range(1, n):
        up.append(lax.ppermute(up[-1], "gy", [(j, j + 1) for j in range(t - 1, n - 1)]))
        back.append(lax.ppermute(back[-1], "gy", [(j, j - 1) for j in range(1, n - t + 1)]))
        yield
        up[-1], back[-1] = turn.take(up[-1], back[-1])
    *send, keep = gate_up(at, first, up, back, *notes, gate_weight, up_weight)
    turn.give(*send, keep)
    come = [swap_core(value, gx) for value in send]
    yield
    *come, keep = turn.take(*come, keep)
    sums = (keep + jnp.stack(come).astype(f32)).reshape(2, ring, part, keep.shape[2])
    pick = lambda j: lax.dynamic_index_in_dim(sums, j % ring, 1, keepdims=False)
    travelling = None
    for s in range(1, ring):
        share = pick(x + ring - s)
        if travelling is not None:
            share = share + travelling.astype(f32)
        share = share.astype(bf16)
        turn.give(share)
        travelling = rotate(share, "gx", ring, CORES, 1)
        yield
        (travelling,) = turn.take(travelling)
    mine = pick(x) + travelling.astype(f32)
    hidden = (jax.nn.silu(mine[0]) * mine[1]).astype(bf16)
    turn.give(hidden)
    mine, other = [hidden], []
    for s in range(1, ring):
        mine.append(rotate(mine[-1], "gx", ring, CORES, 1))
        other.append(swap_core(mine[-2], gx))
        yield
        (mine[-1],) = turn.take(mine[-1])
    other.append(swap_core(mine[-1], gx))
    yield
    other = turn.take(*other)
    terms, ahead, behind = down(at, mine, other, down_weight, n)
    turn.give(ahead, behind)
    pick = lambda j: lax.dynamic_index_in_dim(terms, jnp.clip(j, 0, n - 1), 0, keepdims=False)
    for o in range(n - 1, 0, -1):
        if o < n - 1:
            ahead = (pick(place + o) + ahead.astype(f32)).astype(bf16)
            behind = (pick(place - o) + behind.astype(f32)).astype(bf16)
            turn.give(ahead, behind)
        ahead = lax.ppermute(ahead, "gy", [(j, j + 1) for j in range(n - o)])
        behind = lax.ppermute(behind, "gy", [(j, j - 1) for j in range(o, n)])
        yield
        ahead, behind = turn.take(ahead, behind)
    total = (pick(place) + ahead.astype(f32) + behind.astype(f32)).astype(bf16)
    turn.give(total)
    outputs[first] = total


def note_blocks(turn, gx, n, tokens, norm_gain, notes):
    ring = gx // CORES
    rows = tokens.shape[0]
    (values,) = turn.take(tokens)
    values = values.astype(f32)
    squares = jnp.sum(values * values, axis=1)
    turn.give(squares)
    other = swap_core(squares, gx)
    yield
    squares, other = turn.take(squares, other)
    squares = squares + other
    turn.give(squares)
    others = [rotate(squares, "gx", ring, CORES, by) for by in range(1, ring)]
    yield
    squares, *others = turn.take(squares, *others)
    note = jnp.concatenate([squares + sum(others), norm_gain.astype(f32)])
    turn.give(note)
    found = [note] + [rotate(note, "gy", n, 1, t) for t in range(1, n)]
    yield
    found = turn.take(*found)
    scale = lax.rsqrt(sum(note[:rows] for note in found) / D + epsilon)[:, None]
    gain = jnp.stack([note[rows:] for note in found])
    turn.give(scale, gain)
    notes.extend((scale, gain))


def local(gx, n, tokens, norm_gain, gate_weight, up_weight, down_weight):
    micro_count, row_count, width = tokens.shape
    rows = micro_count * row_count
    place, index = lax.axis_index("gy"), lax.axis_index("gx")
    at = jnp.stack([place, lax.rem(index, CORES), lax.div(index, CORES)]).astype(jnp.int32)
    tokens = tokens.reshape(rows, width)
    weights = gate_weight, up_weight, down_weight

    turn, notes, outputs = Turn(), [], {}
    chunks, first = [], 0
    for size in CHUNKS if rows == sum(CHUNKS) else (rows,):
        chunks.append(chunk_blocks(turn, gx, n, at, first, size, tokens, notes, weights, outputs))
        first += size
    noting = note_blocks(turn, gx, n, tokens, norm_gain, notes)
    next(chunks[0], None)
    next(noting, None)
    next(noting, None)
    next(chunks[0], None)
    next(noting, None)
    next(chunks[0], None)
    next(noting, None)
    if (n, gx) == (4, 4) and len(chunks) == len(CHUNKS):
        for c in ORDER:
            next(chunks[c], None)
    for chunk in chunks:
        for _ in chunk:
            pass
    return jnp.concatenate([outputs[f] for f in sorted(outputs)]).reshape(micro_count, row_count, width)


def solution(mesh):
    in_specs = (
        P(None, "groups", ("gx", "gy")),
        P(("gx", "gy")),
        P("gx", "gy"),
        P("gx", "gy"),
        P("gy", "gx"),
    )
    out_specs = P(None, "groups", ("gx", "gy"))
    return jax.shard_map(
        functools.partial(local, mesh.shape["gx"], mesh.shape["gy"]),
        mesh=mesh,
        in_specs=in_specs,
        out_specs=out_specs,
        check_vma=False,
    )
```

```python
import functools

import jax
import jax.numpy as jnp
from jax import lax
from jax.experimental import pallas as pl
from jax.experimental.pallas import tpu as pltpu
from jax.sharding import PartitionSpec as P

D = 18432
CHUNKS = (384, 384, 256)
ORDER = (1, 0, 1, 0, 0, 2, 1, 1, 0, 2, 1, 0, 2, 1, 2, 0, 2, 1, 2, 0, 1, 2, 0, 2, 1, 2, 1, 2, 1, 2)
VMEM = 48 * 1024 * 1024
bf16, f32 = jnp.bfloat16, jnp.float32
PAIRS = [(0, 1), (1, 0), (2, 3), (3, 2)]
MIDDLE = [(1, 2), (2, 1)]
INWARD = [(0, 1), (3, 2)]
OUTWARD = [(1, 0), (2, 3)]
SWAP_CORE = [(0, 1), (1, 0), (2, 3), (3, 2)]
SWAP_X = [(0, 2), (1, 3), (2, 0), (3, 1)]
PLACE, CORE, X, SIDE, TWIN = range(5)


epsilon = 1e-05


def kernel_call(body, grid, ins, outs, shapes, scratch, name):
    return pl.pallas_call(
        body,
        grid_spec=pltpu.PrefetchScalarGridSpec(
            num_scalar_prefetch=1, grid=(grid,), in_specs=ins, out_specs=outs, scratch_shapes=scratch
        ),
        out_shape=[jax.ShapeDtypeStruct(*shape) for shape in shapes],
        compiler_params=pltpu.CompilerParams(vmem_limit_bytes=VMEM),
        cost_estimate=pl.CostEstimate(flops=0, bytes_accessed=0, transcendentals=0),
        name=name,
    )


def whole(*shape):
    return pl.BlockSpec(shape, lambda j, at: (0,) * len(shape))


def normalize(at, rows, shard, source, scale, gain, normed, column):
    behind = lax.rem(at[PLACE] + 4 - shard, 4)
    values = source[...].astype(f32) * scale[rows, :] * gain[pl.ds(behind, 1), :]
    normed[:, pl.ds(column, source.shape[1])] = values.astype(bf16)


def early_kernel(rows, at, own, pair, inner, outer, scale, gain, *refs):
    weights, sums, normed = refs[:6], refs[6], refs[7]
    width = own.shape[1]
    place, side = at[PLACE], at[SIDE]

    @pl.when(pl.program_id(0) == 0)
    def _():
        def fill(shard, source):
            column = pl.multiple_of((shard - side) * width, 128)
            normalize(at, rows, shard, source, scale, gain, normed, column)

        fill(place, own)
        fill(at[TWIN], pair)
        middle = (place == 1) | (place == 2)
        pl.when(middle)(lambda: fill(2 - side, inner))
        pl.when(jnp.logical_not(middle))(lambda: fill(2 - side, outer))

    for k in range(2):
        total = None
        for m in range(3):
            term = jnp.dot(
                normed[:, m * width : (m + 1) * width], weights[3 * k + m][...], preferred_element_type=f32
            )
            total = term if total is None else total + term
        sums[k] = total


def early(at, rows, own, pair, inner, outer, scale, gain, gate_weight, up_weight):
    size, width = own.shape
    cols = gate_weight.shape[1]
    tile = 256
    blocks = [pl.BlockSpec((width, tile), lambda j, at, m=m: (at[SIDE] + m, j)) for m in range(3)]
    return kernel_call(
        functools.partial(early_kernel, rows),
        cols // tile,
        [whole(size, width)] * 4 + [whole(*scale.shape), whole(*gain.shape)] + blocks * 2,
        [pl.BlockSpec((2, size, tile), lambda j, at: (0, 0, j))],
        [((2, size, cols), f32)],
        [pltpu.VMEM((size, 3 * width), bf16)],
        "early",
    )(at, own, pair, inner, outer, scale, gain, *[gate_weight] * 3, *[up_weight] * 3)[0]


def late_kernel(rows, at, inner, outer, scale, gain, gate_w, up_w, sums, send_gate, send_up, keep, normed, product):
    place, core, far = at[PLACE], at[CORE], 3 - 3 * at[SIDE]
    half = keep.shape[1]

    @pl.when(pl.program_id(0) == 0)
    def _():
        middle = (place == 1) | (place == 2)
        fill = lambda source: normalize(at, rows, far, source, scale, gain, normed, 0)
        pl.when(middle)(lambda: fill(inner))
        pl.when(jnp.logical_not(middle))(lambda: fill(outer))

    for k, (weight, send) in enumerate(((gate_w, send_gate), (up_w, send_up))):
        product[...] = sums[k] + jnp.dot(normed[...], weight[...], preferred_element_type=f32)
        send[...] = product[pl.ds(pl.multiple_of((1 - core) * half, 16), half), :].astype(bf16)
        keep[k] = product[pl.ds(pl.multiple_of(core * half, 16), half), :]


def late(at, rows, inner, outer, scale, gain, gate_weight, up_weight, sums):
    size, width = inner.shape
    cols = gate_weight.shape[1]
    half, tile = size // 2, cols // 3
    block = pl.BlockSpec((width, tile), lambda j, at: (3 - 3 * at[SIDE], j))
    away = pl.BlockSpec((half, tile), lambda j, at: (0, j))
    return kernel_call(
        functools.partial(late_kernel, rows),
        cols // tile,
        [whole(size, width)] * 2
        + [whole(*scale.shape), whole(*gain.shape), block, block]
        + [pl.BlockSpec((2, size, tile), lambda j, at: (0, 0, j))],
        [away, away, pl.BlockSpec((2, half, tile), lambda j, at: (0, 0, j))],
        [((half, cols), bf16), ((half, cols), bf16), ((2, half, cols), f32)],
        [pltpu.VMEM((size, width), bf16), pltpu.VMEM((size, tile), f32)],
        "late",
    )(at, inner, outer, scale, gain, gate_weight, up_weight, sums)


def sum_kernel(at, keep, gate, up, share, mine):
    x, part = at[X], share.shape[1]
    for k, come in enumerate((gate, up)):
        for quarter, out in ((1 - x, share), (x, mine)):
            rows = pl.ds(pl.multiple_of(quarter * part, 16), part)
            out[k] = (keep[k, rows, :] + come[rows, :].astype(f32)).astype(out.dtype)


def add_core(at, keep, gate, up):
    _, half, cols = keep.shape
    part, tile = half // 2, cols // 3
    piece = lambda *shape: pl.BlockSpec((*shape, tile), lambda j, at: (0,) * len(shape) + (j,))
    return kernel_call(
        sum_kernel,
        cols // tile,
        [piece(2, half), piece(half), piece(half)],
        [piece(2, part), piece(2, part)],
        [((2, part, cols), bf16), ((2, part, cols), f32)],
        [],
        "add_core",
    )(at, keep, gate, up)


def down_kernel(at, near, far, weight, terms, ahead, hidden):
    x = at[X]
    part = near.shape[0] // 2

    @pl.when(pl.program_id(0) == 0)
    def _():
        for core in range(2):
            for quarter, pieces in ((2 * core + x, near), (2 * core + 1 - x, far)):
                row = pl.multiple_of(quarter * part, 16)
                hidden[pl.ds(row, part), :] = pieces[core * part : (core + 1) * part, :]

    product = jnp.dot(hidden[...], weight[...], preferred_element_type=f32)
    terms[0] = product

    @pl.when(pl.program_id(0) == 3 - at[PLACE])
    def _():
        ahead[...] = product.astype(bf16)


def down(at, near, far, down_weight):
    both, depth = near.shape
    size, width = 2 * both, down_weight.shape[1] // 4
    return kernel_call(
        down_kernel,
        4,
        [whole(both, depth)] * 2 + [pl.BlockSpec((depth, width), lambda j, at: (0, j))],
        [pl.BlockSpec((1, size, width), lambda j, at: (j, 0, 0)), whole(size, width)],
        [((4, size, width), f32), ((size, width), bf16)],
        [pltpu.VMEM((size, depth), bf16)],
        "down",
    )(at, near, far, down_weight)


class Turn:
    def __init__(self):
        self.held = ()

    def take(self, *values):
        values, _ = lax.optimization_barrier((values, self.held))
        self.held = values
        return values

    def give(self, *values):
        self.held = values


def chunk_blocks(turn, at, first, size, tokens, notes, weights, outputs):
    gate_weight, up_weight, down_weight = weights
    place = at[PLACE]
    rows = slice(first, first + size)
    along = lambda value, pairs: lax.ppermute(value, "gy", pairs)

    (own,) = turn.take(tokens[rows])
    pair, inner = along(own, PAIRS), along(own, MIDDLE)
    yield
    pair, inner = turn.take(pair, inner)
    far_inner, outer = along(pair, MIDDLE), along(inner, OUTWARD)
    yield
    far_inner, outer = turn.take(far_inner, outer)
    far_outer = along(far_inner, OUTWARD)
    yield
    own, pair, inner, outer = turn.take(own, pair, inner, outer)
    sums = early(at, rows, own, pair, inner, outer, *notes, gate_weight, up_weight)
    turn.give(sums)
    yield
    far_outer, sums = turn.take(far_outer, sums)
    *send, keep = late(at, rows, far_inner, far_outer, *notes, gate_weight, up_weight, sums)
    turn.give(*send, keep)

    come = [lax.ppermute(value, "gx", SWAP_CORE) for value in send]
    yield
    *come, keep = turn.take(*come, keep)
    share, mine = add_core(at, keep, *come)
    turn.give(share, mine)
    come = lax.ppermute(share, "gx", SWAP_X)
    yield
    come, mine = turn.take(come, mine)
    mine = mine + come.astype(f32)
    hidden = (jax.nn.silu(mine[0]) * mine[1]).astype(bf16)
    turn.give(hidden)
    cores = lambda value: lax.all_gather(value, "gx", axis_index_groups=[[0, 1], [2, 3]], axis=0, tiled=True)
    far, near = lax.ppermute(hidden, "gx", SWAP_X), cores(hidden)
    yield
    far, near = turn.take(far, near)
    terms, ahead = down(at, near, cores(far), down_weight)
    turn.give(ahead)

    pick = lambda j: lax.dynamic_index_in_dim(terms, j, 0, keepdims=False)
    from_end = along(ahead, INWARD)
    yield
    (from_end,) = turn.take(from_end)
    second = (pick((place + 2) % 4) + from_end.astype(f32)).astype(bf16)
    turn.give(second)
    to_middle, to_far = along(second, INWARD), along(second, MIDDLE)
    yield
    to_middle, to_far = turn.take(to_middle, to_far)
    third = (pick(at[TWIN]) + to_far.astype(f32)).astype(bf16)
    fourth = (pick(3 - place) + to_middle.astype(f32)).astype(bf16)
    turn.give(third, fourth)
    third, fourth = along(third, PAIRS), along(fourth, MIDDLE)
    yield
    third, fourth = turn.take(third, fourth)
    total = (pick(place) + third.astype(f32) + fourth.astype(f32)).astype(bf16)
    turn.give(total)
    outputs[first] = total


def note_blocks(turn, tokens, norm_gain, notes):
    rows = tokens.shape[0]
    (values,) = turn.take(tokens)
    values = values.astype(f32)
    squares = jnp.sum(values * values, axis=1)
    turn.give(squares)
    other = lax.ppermute(squares, "gx", SWAP_CORE)
    yield
    squares, other = turn.take(squares, other)
    squares = squares + other
    turn.give(squares)
    other = lax.ppermute(squares, "gx", SWAP_X)
    yield
    squares, other = turn.take(squares, other)
    note = jnp.concatenate([squares + other, norm_gain.astype(f32)])
    turn.give(note)
    found = [note] + [lax.ppermute(note, "gy", [(j, (j + t) % 4) for j in range(4)]) for t in range(1, 4)]
    yield
    found = turn.take(*found)
    scale = lax.rsqrt(sum(note[:rows] for note in found) / D + epsilon)[:, None]
    gain = jnp.stack([note[rows:] for note in found])
    turn.give(scale, gain)
    notes.extend((scale, gain))


def chunked(tokens, norm_gain, *weights):
    place, index = lax.axis_index("gy"), lax.axis_index("gx")
    at = jnp.stack([place, index % 2, index // 2, place // 2, place + 1 - 2 * (place % 2)]).astype(jnp.int32)
    turn, notes, outputs = Turn(), [], {}
    chunks, first = [], 0
    for size in CHUNKS:
        chunks.append(chunk_blocks(turn, at, first, size, tokens, notes, weights, outputs))
        first += size
    noting = note_blocks(turn, tokens, norm_gain, notes)
    for blocks in (chunks[0], noting, noting, chunks[0], noting, chunks[0], noting):
        next(blocks, None)
    for c in ORDER:
        next(chunks[c], None)
    return jnp.concatenate([outputs[f] for f in sorted(outputs)])


def plain(tokens, norm_gain, gate_weight, up_weight, down_weight):
    values = tokens.astype(f32)
    squares = lax.psum(jnp.sum(values * values, axis=1), ("gx", "gy"))
    normed = (
        values * lax.rsqrt(squares / D + epsilon)[:, None] * norm_gain.astype(f32)[None, :]
    ).astype(bf16)
    gathered = lax.all_gather(normed, "gy", axis=1, tiled=True)
    gate, up = (
        lax.psum_scatter(
            jnp.dot(gathered, weight, preferred_element_type=f32), "gx", scatter_dimension=1, tiled=True
        )
        for weight in (gate_weight, up_weight)
    )
    hidden = (jax.nn.silu(gate) * up).astype(bf16)
    terms = jnp.dot(
        lax.all_gather(hidden, "gx", axis=1, tiled=True), down_weight, preferred_element_type=f32
    )
    return lax.psum_scatter(terms, "gy", scatter_dimension=1, tiled=True).astype(bf16)


def local(sizes, tokens, *rest):
    micro_count, row_count, width = tokens.shape
    rows = micro_count * row_count
    form = chunked if sizes == (4, 4) and rows == sum(CHUNKS) and width % 128 == 0 else plain
    return form(tokens.reshape(rows, width), *rest).reshape(tokens.shape)


def solution(mesh):
    in_specs = (
        P(None, "groups", ("gx", "gy")),
        P(("gx", "gy")),
        P("gx", "gy"),
        P("gx", "gy"),
        P("gy", "gx"),
    )
    out_specs = P(None, "groups", ("gx", "gy"))
    return jax.shard_map(
        functools.partial(local, (mesh.shape["gx"], mesh.shape["gy"])),
        mesh=mesh,
        in_specs=in_specs,
        out_specs=out_specs,
        check_vma=False,
    )
```

```python
import functools

import jax
import jax.numpy as jnp
from jax import lax
from jax.experimental import pallas as pl
from jax.experimental.pallas import tpu as pltpu
from jax.sharding import PartitionSpec as P

D = 18432
CHUNKS = (384, 384, 256)
ORDER = (1, 0, 1, 0, 0, 2, 1, 1, 0, 2, 1, 0, 2, 1, 2, 0, 2, 1, 2, 0, 1, 2, 0, 2, 1, 2, 1, 2, 1, 2)
VMEM = 48 * 1024 * 1024
bf16, f32 = jnp.bfloat16, jnp.float32
PAIRS = [(0, 1), (1, 0), (2, 3), (3, 2)]
MIDDLE = [(1, 2), (2, 1)]
INWARD = [(0, 1), (3, 2)]
OUTWARD = [(1, 0), (2, 3)]
SWAP_CORE = [(0, 1), (1, 0), (2, 3), (3, 2)]
SWAP_X = [(0, 2), (1, 3), (2, 0), (3, 1)]
PLACE, CORE, X, SIDE, TWIN = range(5)


epsilon = 1e-05


def kernel_call(body, grid, ins, outs, shapes, scratch, name):
    return pl.pallas_call(
        body,
        grid_spec=pltpu.PrefetchScalarGridSpec(
            num_scalar_prefetch=1, grid=(grid,), in_specs=ins, out_specs=outs, scratch_shapes=scratch
        ),
        out_shape=[jax.ShapeDtypeStruct(*shape) for shape in shapes],
        compiler_params=pltpu.CompilerParams(vmem_limit_bytes=VMEM),
        cost_estimate=pl.CostEstimate(flops=0, bytes_accessed=0, transcendentals=0),
        name=name,
    )


def whole(*shape):
    return pl.BlockSpec(shape, lambda j, at: (0,) * len(shape))


def normalize(at, rows, shard, source, scale, gain, normed, column):
    behind = lax.rem(at[PLACE] + 4 - shard, 4)
    values = source[...].astype(f32) * scale[rows, :] * gain[pl.ds(behind, 1), :]
    normed[:, pl.ds(column, source.shape[1])] = values.astype(bf16)


def early_kernel(rows, at, own, pair, inner, outer, scale, gain, *refs):
    gate_w, up_w, sums, normed = refs
    width = own.shape[1]
    place, side = at[PLACE], at[SIDE]

    @pl.when(pl.program_id(0) == 0)
    def _():
        def fill(shard, source):
            column = pl.multiple_of((shard - side) * width, 128)
            normalize(at, rows, shard, source, scale, gain, normed, column)

        fill(place, own)
        fill(at[TWIN], pair)
        middle = (place == 1) | (place == 2)
        pl.when(middle)(lambda: fill(2 - side, inner))
        pl.when(jnp.logical_not(middle))(lambda: fill(2 - side, outer))

    for k, weight in enumerate((gate_w, up_w)):
        sums[k] = jnp.dot(normed[...], weight[...], preferred_element_type=f32)


def early(at, rows, own, pair, inner, outer, scale, gain, gate_weight, up_weight):
    size, width = own.shape
    cols = gate_weight.shape[1]
    tile = 256
    block = pl.BlockSpec(
        (pl.Element(3 * width), pl.Element(tile)), lambda j, at: (at[SIDE] * width, j * tile)
    )
    return kernel_call(
        functools.partial(early_kernel, rows),
        cols // tile,
        [whole(size, width)] * 4 + [whole(*scale.shape), whole(*gain.shape), block, block],
        [pl.BlockSpec((2, size, tile), lambda j, at: (0, 0, j))],
        [((2, size, cols), f32)],
        [pltpu.VMEM((size, 3 * width), bf16)],
        "early",
    )(at, own, pair, inner, outer, scale, gain, gate_weight, up_weight)[0]


def late_kernel(rows, at, inner, outer, scale, gain, gate_w, up_w, sums, send_gate, send_up, keep, normed, product):
    place, core, far = at[PLACE], at[CORE], 3 - 3 * at[SIDE]
    half = keep.shape[1]

    @pl.when(pl.program_id(0) == 0)
    def _():
        middle = (place == 1) | (place == 2)
        fill = lambda source: normalize(at, rows, far, source, scale, gain, normed, 0)
        pl.when(middle)(lambda: fill(inner))
        pl.when(jnp.logical_not(middle))(lambda: fill(outer))

    for k, (weight, send) in enumerate(((gate_w, send_gate), (up_w, send_up))):
        product[...] = sums[k] + jnp.dot(normed[...], weight[...], preferred_element_type=f32)
        send[...] = product[pl.ds(pl.multiple_of((1 - core) * half, 16), half), :].astype(bf16)
        keep[k] = product[pl.ds(pl.multiple_of(core * half, 16), half), :]


def late(at, rows, inner, outer, scale, gain, gate_weight, up_weight, sums):
    size, width = inner.shape
    cols = gate_weight.shape[1]
    half, tile = size // 2, 256
    block = pl.BlockSpec((width, tile), lambda j, at: (3 - 3 * at[SIDE], j))
    away = pl.BlockSpec((half, tile), lambda j, at: (0, j))
    return kernel_call(
        functools.partial(late_kernel, rows),
        cols // tile,
        [whole(size, width)] * 2
        + [whole(*scale.shape), whole(*gain.shape), block, block]
        + [pl.BlockSpec((2, size, tile), lambda j, at: (0, 0, j))],
        [away, away, pl.BlockSpec((2, half, tile), lambda j, at: (0, 0, j))],
        [((half, cols), bf16), ((half, cols), bf16), ((2, half, cols), f32)],
        [pltpu.VMEM((size, width), bf16), pltpu.VMEM((size, tile), f32)],
        "late",
    )(at, inner, outer, scale, gain, gate_weight, up_weight, sums)


def sum_kernel(at, keep, gate, up, share, mine):
    x, part = at[X], share.shape[1]
    for k, come in enumerate((gate, up)):
        for quarter, out in ((1 - x, share), (x, mine)):
            rows = pl.ds(pl.multiple_of(quarter * part, 16), part)
            out[k] = (keep[k, rows, :] + come[rows, :].astype(f32)).astype(out.dtype)


def add_core(at, keep, gate, up):
    _, half, cols = keep.shape
    part, tile = half // 2, cols // 3
    piece = lambda *shape: pl.BlockSpec((*shape, tile), lambda j, at: (0,) * len(shape) + (j,))
    return kernel_call(
        sum_kernel,
        cols // tile,
        [piece(2, half), piece(half), piece(half)],
        [piece(2, part), piece(2, part)],
        [((2, part, cols), bf16), ((2, part, cols), f32)],
        [],
        "add_core",
    )(at, keep, gate, up)


def down_kernel(at, near, far, weight, terms, ahead, hidden):
    x = at[X]
    part = near.shape[0] // 2

    @pl.when(pl.program_id(0) == 0)
    def _():
        for core in range(2):
            for quarter, pieces in ((2 * core + x, near), (2 * core + 1 - x, far)):
                row = pl.multiple_of(quarter * part, 16)
                hidden[pl.ds(row, part), :] = pieces[core * part : (core + 1) * part, :]

    product = jnp.dot(hidden[...], weight[...], preferred_element_type=f32)
    terms[0] = product

    @pl.when(pl.program_id(0) == 3 - at[PLACE])
    def _():
        ahead[...] = product.astype(bf16)


def down(at, near, far, down_weight):
    both, depth = near.shape
    size, width = 2 * both, down_weight.shape[1] // 4
    return kernel_call(
        down_kernel,
        4,
        [whole(both, depth)] * 2 + [pl.BlockSpec((depth, width), lambda j, at: (0, j))],
        [pl.BlockSpec((1, size, width), lambda j, at: (j, 0, 0)), whole(size, width)],
        [((4, size, width), f32), ((size, width), bf16)],
        [pltpu.VMEM((size, depth), bf16)],
        "down",
    )(at, near, far, down_weight)


class Turn:
    def __init__(self):
        self.held = ()

    def take(self, *values):
        values, _ = lax.optimization_barrier((values, self.held))
        self.held = values
        return values

    def give(self, *values):
        self.held = values


def chunk_blocks(turn, at, first, size, tokens, notes, weights, outputs):
    gate_weight, up_weight, down_weight = weights
    place = at[PLACE]
    rows = slice(first, first + size)
    along = lambda value, pairs: lax.ppermute(value, "gy", pairs)

    (own,) = turn.take(tokens[rows])
    pair, inner = along(own, PAIRS), along(own, MIDDLE)
    yield
    pair, inner = turn.take(pair, inner)
    far_inner, outer = along(pair, MIDDLE), along(inner, OUTWARD)
    yield
    far_inner, outer = turn.take(far_inner, outer)
    far_outer = along(far_inner, OUTWARD)
    yield
    own, pair, inner, outer = turn.take(own, pair, inner, outer)
    sums = early(at, rows, own, pair, inner, outer, *notes, gate_weight, up_weight)
    turn.give(sums)
    yield
    far_outer, sums = turn.take(far_outer, sums)
    *send, keep = late(at, rows, far_inner, far_outer, *notes, gate_weight, up_weight, sums)
    turn.give(*send, keep)

    come = [lax.ppermute(value, "gx", SWAP_CORE) for value in send]
    yield
    *come, keep = turn.take(*come, keep)
    share, mine = add_core(at, keep, *come)
    turn.give(share, mine)
    come = lax.ppermute(share, "gx", SWAP_X)
    yield
    come, mine = turn.take(come, mine)
    mine = mine + come.astype(f32)
    hidden = (jax.nn.silu(mine[0]) * mine[1]).astype(bf16)
    turn.give(hidden)
    cores = lambda value: lax.all_gather(value, "gx", axis_index_groups=[[0, 1], [2, 3]], axis=0, tiled=True)
    far, near = lax.ppermute(hidden, "gx", SWAP_X), cores(hidden)
    yield
    far, near = turn.take(far, near)
    terms, ahead = down(at, near, cores(far), down_weight)
    turn.give(ahead)

    pick = lambda j: lax.dynamic_index_in_dim(terms, j, 0, keepdims=False)
    from_end = along(ahead, INWARD)
    yield
    (from_end,) = turn.take(from_end)
    second = (pick((place + 2) % 4) + from_end.astype(f32)).astype(bf16)
    turn.give(second)
    to_middle, to_far = along(second, INWARD), along(second, MIDDLE)
    yield
    to_middle, to_far = turn.take(to_middle, to_far)
    third = (pick(at[TWIN]) + to_far.astype(f32)).astype(bf16)
    fourth = (pick(3 - place) + to_middle.astype(f32)).astype(bf16)
    turn.give(third, fourth)
    third, fourth = along(third, PAIRS), along(fourth, MIDDLE)
    yield
    third, fourth = turn.take(third, fourth)
    total = (pick(place) + third.astype(f32) + fourth.astype(f32)).astype(bf16)
    turn.give(total)
    outputs[first] = total


def note_blocks(turn, tokens, norm_gain, notes):
    rows = tokens.shape[0]
    (values,) = turn.take(tokens)
    values = values.astype(f32)
    squares = jnp.sum(values * values, axis=1)
    turn.give(squares)
    other = lax.ppermute(squares, "gx", SWAP_CORE)
    yield
    squares, other = turn.take(squares, other)
    squares = squares + other
    turn.give(squares)
    other = lax.ppermute(squares, "gx", SWAP_X)
    yield
    squares, other = turn.take(squares, other)
    note = jnp.concatenate([squares + other, norm_gain.astype(f32)])
    turn.give(note)
    found = [note] + [lax.ppermute(note, "gy", [(j, (j + t) % 4) for j in range(4)]) for t in range(1, 4)]
    yield
    found = turn.take(*found)
    scale = lax.rsqrt(sum(note[:rows] for note in found) / D + epsilon)[:, None]
    gain = jnp.stack([note[rows:] for note in found])
    turn.give(scale, gain)
    notes.extend((scale, gain))


def chunked(tokens, norm_gain, *weights):
    place, index = lax.axis_index("gy"), lax.axis_index("gx")
    at = jnp.stack([place, index % 2, index // 2, place // 2, place + 1 - 2 * (place % 2)]).astype(jnp.int32)
    turn, notes, outputs = Turn(), [], {}
    chunks, first = [], 0
    for size in CHUNKS:
        chunks.append(chunk_blocks(turn, at, first, size, tokens, notes, weights, outputs))
        first += size
    noting = note_blocks(turn, tokens, norm_gain, notes)
    for blocks in (chunks[0], noting, noting, chunks[0], noting, chunks[0], noting):
        next(blocks, None)
    for c in ORDER:
        next(chunks[c], None)
    return jnp.concatenate([outputs[f] for f in sorted(outputs)])


def plain(tokens, norm_gain, gate_weight, up_weight, down_weight):
    values = tokens.astype(f32)
    squares = lax.psum(jnp.sum(values * values, axis=1), ("gx", "gy"))
    normed = (
        values * lax.rsqrt(squares / D + epsilon)[:, None] * norm_gain.astype(f32)[None, :]
    ).astype(bf16)
    gathered = lax.all_gather(normed, "gy", axis=1, tiled=True)
    gate, up = (
        lax.psum_scatter(
            jnp.dot(gathered, weight, preferred_element_type=f32), "gx", scatter_dimension=1, tiled=True
        )
        for weight in (gate_weight, up_weight)
    )
    hidden = (jax.nn.silu(gate) * up).astype(bf16)
    terms = jnp.dot(
        lax.all_gather(hidden, "gx", axis=1, tiled=True), down_weight, preferred_element_type=f32
    )
    return lax.psum_scatter(terms, "gy", scatter_dimension=1, tiled=True).astype(bf16)


def local(sizes, tokens, *rest):
    micro_count, row_count, width = tokens.shape
    rows = micro_count * row_count
    form = chunked if sizes == (4, 4) and rows == sum(CHUNKS) and width % 128 == 0 else plain
    return form(tokens.reshape(rows, width), *rest).reshape(tokens.shape)


def solution(mesh):
    in_specs = (
        P(None, "groups", ("gx", "gy")),
        P(("gx", "gy")),
        P("gx", "gy"),
        P("gx", "gy"),
        P("gy", "gx"),
    )
    out_specs = P(None, "groups", ("gx", "gy"))
    return jax.shard_map(
        functools.partial(local, (mesh.shape["gx"], mesh.shape["gy"])),
        mesh=mesh,
        in_specs=in_specs,
        out_specs=out_specs,
        check_vma=False,
    )
```
